1024 devices in a mesh: group: 16 (over z_lo), local: 64 (over x, z_hi, y, core).
Axes of the slice: x: 4, y: 4, z: 32 (z_hi: 2, z_lo: 16; z = z_hi * 16 + z_lo), core: 2. Of those that a mesh axis runs over, the one named last changes fastest.
Arguments:
- inputs: bfloat16 [131072, 2048], P(('group', 'local')), may hold values from -24 to 24
- out_grad: bfloat16 [131072, 2048], P(('group', 'local')), may hold values from -24 to 24
- routes: int32 [131072, 2], P(('group', 'local')), may hold values from 0 to 127, as said below
- router_weight: bfloat16 [2048, 128], replicated, may hold values from -0.25 to 0.25
- w_in: bfloat16 [2048, 32768], P(None, 'local'), may hold values from -0.125 to 0.125
- w_out: bfloat16 [32768, 2048], P('local'), may hold values from -0.0625 to 0.0625
Outputs:
- in_grad: bfloat16 [131072, 2048], P(('group', 'local'))
- w_in_grad: bfloat16 [2048, 32768], P('group', 'local')
- w_out_grad: bfloat16 [32768, 2048], P('local', 'group')
The draws below stay inside these ranges and needn't reach their ends.
Inputs may be any that keep to these rules, and one draw needn't show every extreme that they name: `routes`: the two experts of a token differ. Among the 128 tokens of one device at most 4 name any one expert below 4.
All inputs are finite; a program needn't handle non-finite values.
Results may differ from the reference program's by a relative error of at most 0.023.
Values may be sent and summed in bfloat16 or wider, within the bound.
No kernel may reach another device: no remote copies, remote signals or barrier semaphores. Data moves between devices by JAX's collectives and lax.ppermute only.
A program may use at most 32 MiB of HBM per device.

```python
import jax
import jax.numpy as jnp
from jax import lax

D = 2048
FF = 8192
EXPERTS = 128
TOPK = 2
CAP = 4
TOK_DEV = 128
EXP_WIN = 4
SPLIT = 16
FF_DEV = 512
TOKENS = 131072
N_GROUP = 16
N_LOCAL = 64


def draw_routes(key, part):
    key = jax.random.fold_in(key, 11)
    keys = jax.random.split(key, 8)
    blocks = TOKENS // TOK_DEV
    counts = jax.random.randint(keys[0], (blocks, EXP_WIN), 0, CAP + 1)
    fullest = jax.random.randint(keys[1], (EXP_WIN,), 0, blocks)
    block_ids = jnp.arange(blocks, dtype=jnp.int32)
    expert_ids = jnp.arange(EXP_WIN, dtype=jnp.int32)
    full_group = jax.random.randint(keys[2], (), 0, N_GROUP)
    full_expert = jax.random.randint(keys[3], (), 0, EXP_WIN)
    forced = (block_ids[:, None] == fullest[None, :]) | (block_ids[:, None] // N_LOCAL == full_group) & (expert_ids[None, :] == full_expert)
    counts = jnp.where(forced, CAP, counts)
    starts = jnp.cumsum(counts, axis=1) - counts
    ranks = jax.vmap(lambda one: jax.random.permutation(one, TOK_DEV))(jax.random.split(keys[4], blocks))
    inside = (ranks[:, :, None] >= starts[:, None, :]) & (ranks[:, :, None] < starts[:, None, :] + counts[:, None, :])
    takes = jnp.any(inside, axis=2)
    which = jnp.sum(inside.astype(jnp.int32) * expert_ids[None, None, :], axis=2)
    others = EXPERTS - EXP_WIN
    first = jax.random.randint(keys[5], (blocks, TOK_DEV), EXP_WIN, EXPERTS)
    offset = jax.random.randint(keys[6], (blocks, TOK_DEV), 1, others)
    second = EXP_WIN + (first - EXP_WIN + offset) % others
    left = jnp.where(takes, which, first)
    right = jnp.where(takes, first, second)
    flips = jax.random.randint(keys[7], (blocks, TOK_DEV), 0, 2) == 1
    col_a = jnp.where(flips, right, left)
    col_b = jnp.where(flips, left, right)
    return jnp.stack([col_a, col_b], axis=-1).reshape(TOKENS, TOPK).astype(jnp.int32)


def raised(result, rng, source, target, shards_of, factor):
    owner, partner = [(jnp.arange(result.shape[axis_at]) // (result.shape[axis_at] // shards_of)).reshape([-1 if axis == axis_at else 1 for axis in range(result.ndim)]) for axis_at in (source, target)]
    chosen = jax.random.permutation(rng, shards_of)[partner]
    strong = (owner == chosen) | (owner == (partner + shards_of // 2) % shards_of)
    return jnp.where(strong, factor * result, result)


def block_scale(stream_key, extent, cuts, low, top_value):
    loudness, own = 1.0, jax.random.fold_in(stream_key, 6)
    for dim, parts in cuts:
        draws = jnp.exp(jax.random.uniform(jax.random.fold_in(own, dim), (parts,), jnp.float32, low / len(cuts), top_value / len(cuts)))
        loudness = loudness * jnp.repeat(draws, extent[dim] // parts).reshape([-1 if axis == dim else 1 for axis in range(len(extent))])
    return loudness


def bell_draw(rng, dims, spread, limit, cuts=(), kind=jnp.bfloat16):
    drawn = spread * jax.random.normal(rng, dims, jnp.float32)
    if cuts:
        drawn = drawn * block_scale(rng, dims, cuts, -0.22, 0.18)
    return jnp.clip(drawn, -limit, limit).astype(kind)


def bell_draw_with(own_key, shape, width, bound, shards, heavy, kind=jnp.bfloat16):
    drawn = width * jax.random.normal(own_key, shape, jnp.float32)
    if shards:
        drawn = drawn * block_scale(own_key, shape, shards, -0.22, 0.18)
    return jnp.clip(raised(drawn, jax.random.fold_in(own_key, 3), *heavy), -bound, bound).astype(kind)


def setup_inputs(seed: int = 0) -> dict:
    seeds = jax.random.split(jax.random.key(seed), 7)
    inputs = bell_draw_with(seeds[0], (TOKENS, D), 1.0, 24.0, ((0, 1024),), (0, 1, 1024, 6.0))
    out_grad = bell_draw_with(seeds[1], (TOKENS, D), 1.0, 24.0, ((0, 1024),), (0, 1, 1024, 6.0))
    routes = draw_routes(jax.random.fold_in(seeds[6], 71), 0)
    router_weight = bell_draw(seeds[3], (D, EXPERTS), (D // 4) ** -0.5, 0.25)
    w_in = bell_draw(seeds[4], (D, EXP_WIN * FF), D ** -0.5, 0.125, ((1, 64),))
    w_out = bell_draw(seeds[5], (EXP_WIN * FF, D), FF ** -0.5, 0.0625, ((0, 64),))
    return {"inputs": inputs, "out_grad": out_grad, "routes": routes, "router_weight": router_weight, "w_in": w_in, "w_out": w_out}


gelu_c = 0.7978845608
gelu_a = 0.044715


def gelu_pair(pre_act):
    inner = gelu_c * (pre_act + gelu_a * pre_act * pre_act * pre_act)
    tval = jnp.tanh(inner)
    value = 0.5 * pre_act * (1.0 + tval)
    slope = 0.5 * (1.0 + tval) + 0.5 * pre_act * (1.0 - tval * tval) * gelu_c * (1.0 + 3.0 * gelu_a * pre_act * pre_act)
    return value, slope


def round_trip(values):
    return lax.optimization_barrier(values.astype(jnp.bfloat16)).astype(jnp.float32)


def reference(inputs, out_grad, routes, router_weight, w_in, w_out):
    logits = jnp.dot(inputs, router_weight, preferred_element_type=jnp.float32)
    chosen = jnp.take_along_axis(logits, routes, axis=1)
    gate_vals = 1.0 / (1.0 + jnp.exp(chosen[:, ::-1] - chosen))
    scaled = (gate_vals[:, :, None] * out_grad.astype(jnp.float32)[:, None, :]).astype(jnp.bfloat16)
    blocks = TOKENS // TOK_DEV
    route_rows = TOK_DEV * TOPK
    group_rows = N_LOCAL * CAP
    flat_routes = routes.reshape(blocks, route_rows)
    slot_ids = jnp.arange(CAP, dtype=jnp.int32)
    zero_rows = jnp.zeros((blocks, CAP, D), jnp.bfloat16)
    grad_total = jnp.zeros((blocks, TOK_DEV, D), jnp.float32)
    first_parts = []
    second_parts = []
    for expert in range(EXP_WIN):
        mine = (flat_routes == expert).astype(jnp.int32)
        slot_pos = jnp.cumsum(mine, axis=1) - mine
        picked = ((mine[:, None, :] == 1) & (slot_pos[:, None, :] == slot_ids[None, :, None])).astype(jnp.int32)
        route_of = jnp.sum(picked * jnp.arange(route_rows, dtype=jnp.int32)[None, None, :], axis=2).astype(jnp.int32)
        filled = jnp.sum(picked, axis=2)
        token_of = (route_of // TOPK).astype(jnp.int32)
        xs = jnp.take_along_axis(inputs.reshape(blocks, TOK_DEV, D), token_of[:, :, None], axis=1)
        xs = jnp.where(filled[:, :, None] == 1, xs, zero_rows)
        gs = jnp.take_along_axis(scaled.reshape(blocks, route_rows, D), route_of[:, :, None], axis=1)
        gs = jnp.where(filled[:, :, None] == 1, gs, zero_rows)
        w_first = w_in[:, expert * FF:(expert + 1) * FF]
        w_second = w_out[expert * FF:(expert + 1) * FF, :]
        first_slices = w_first.astype(jnp.float32).reshape(D, SPLIT, FF_DEV)

        def per_group(carry, rows):
            x_rows, g_rows = rows
            pre_act = jnp.dot(x_rows, w_first, preferred_element_type=jnp.float32)
            value, slope = gelu_pair(pre_act)
            hidden = value.astype(jnp.bfloat16)
            hid_grad = (jnp.dot(g_rows, w_second.T, preferred_element_type=jnp.float32) * slope).astype(jnp.bfloat16)
            part_first = jnp.dot(x_rows.T, hid_grad, preferred_element_type=jnp.float32)
            part_second = jnp.dot(hidden.T, g_rows, preferred_element_type=jnp.float32)
            sliced = hid_grad.astype(jnp.float32).reshape(group_rows, SPLIT, FF_DEV)
            partial_value = jnp.einsum("rsf,dsf->rsd", sliced, first_slices, precision=lax.Precision.HIGHEST)
            slot_grad = jnp.sum(round_trip(partial_value), axis=1)
            return (carry[0] + round_trip(part_first), carry[1] + round_trip(part_second)), slot_grad

        start = (jnp.zeros((D, FF), jnp.float32), jnp.zeros((FF, D), jnp.float32))
        sums, slot_grads = lax.scan(per_group, start, (xs.reshape(N_GROUP, group_rows, D), gs.reshape(N_GROUP, group_rows, D)))
        first_parts.append(sums[0].astype(jnp.bfloat16))
        second_parts.append(sums[1].astype(jnp.bfloat16))
        slot_grads = slot_grads.reshape(blocks, CAP, D)
        to_token = ((token_of[:, :, None] == jnp.arange(TOK_DEV, dtype=jnp.int32)[None, None, :]) & (filled[:, :, None] == 1)).astype(jnp.float32)
        grad_total = grad_total + jnp.einsum("bst,bsd->btd", to_token, slot_grads, precision=lax.Precision.HIGHEST)
    in_grad = grad_total.reshape(TOKENS, D).astype(jnp.bfloat16)
    return in_grad, jnp.concatenate(first_parts, axis=1), jnp.concatenate(second_parts, axis=0)
```

```python
import jax
import jax.numpy as jnp
from jax import lax
from jax.sharding import Mesh, PartitionSpec as P

CAP = 4
SPLIT_AXES = (16, 4, 2, 4, 2)
AXES = ("group", "x", "zh", "y", "core")
LOCAL = ("x", "zh", "y", "core")

gelu_c = 0.7978845608
gelu_a = 0.044715


def gelu_pair(pre_act):
    inner = gelu_c * (pre_act + gelu_a * pre_act * pre_act * pre_act)
    tval = jnp.tanh(inner)
    value = 0.5 * pre_act * (1.0 + tval)
    slope = 0.5 * (1.0 + tval) + 0.5 * pre_act * (1.0 - tval * tval) * gelu_c * (
        1.0 + 3.0 * gelu_a * pre_act * pre_act
    )
    return (value, slope)


def dot_f32(a, b, dims):
    return lax.dot_general(a, b, (dims, ((), ())), preferred_element_type=jnp.float32)


def swap(value, axis):
    return lax.ppermute(value, axis, [(0, 1), (1, 0)])


def shift(value, by):
    return lax.ppermute(value, "y", [(i, (i + by) % 4) for i in range(4)])


def slot_rows(inputs, out_grad, routes, router_weight):
    tok_rows = inputs.shape[0]
    n_experts = router_weight.shape[1]
    first, second = routes[:, 0], routes[:, 1]
    expert = lax.broadcasted_iota(jnp.int32, (4, tok_rows), 0)
    mine = (first[None, :] == expert) | (second[None, :] == expert)
    other = jnp.where(mine, first[None, :] + second[None, :] - expert, 0)
    earlier = (
        lax.broadcasted_iota(jnp.int32, (tok_rows, tok_rows), 0)
        < lax.broadcasted_iota(jnp.int32, (tok_rows, tok_rows), 1)
    ).astype(jnp.bfloat16)
    slot_pos = dot_f32(mine.astype(jnp.bfloat16), earlier, ((1,), (0,))).astype(jnp.int32)
    slot_ids = lax.broadcasted_iota(jnp.int32, (4, 2 * CAP, tok_rows), 1) % CAP
    picked = mine[:, None, :] & (slot_pos[:, None, :] == slot_ids)
    sel = picked.reshape(-1, tok_rows)
    other_of = jnp.sum(jnp.where(picked, other[:, None, :], 0), axis=2).reshape(-1)
    sel_bf = sel.astype(jnp.bfloat16)
    x_sel = dot_f32(sel_bf, inputs, ((1,), (0,))).astype(jnp.bfloat16)
    dy_sel = dot_f32(sel_bf, out_grad, ((1,), (0,)))
    logits = dot_f32(x_sel, router_weight, ((1,), (0,)))
    n_rows = sel.shape[0]
    lane = lax.broadcasted_iota(jnp.int32, (n_rows, n_experts), 1)
    row = lax.broadcasted_iota(jnp.int32, (n_rows, n_experts), 0)
    own_logit = jnp.sum(jnp.where(lane == row // (2 * CAP), logits, 0.0), axis=1)
    other_logit = jnp.sum(jnp.where(lane == other_of[:, None], logits, 0.0), axis=1)
    gate = 1.0 / (1.0 + jnp.exp(other_logit - own_logit))
    g_sel = (gate[:, None] * dy_sel).astype(jnp.bfloat16)
    is_x = (lax.broadcasted_iota(jnp.int32, (n_rows, 1), 0) // CAP) % 2 == 0
    return jnp.where(is_x, x_sel, g_sel), sel_bf


def gather_plane(rows):
    pieces = [rows] + [shift(rows, by) for by in (1, 3, 2)]
    own = jnp.concatenate(pieces, axis=1)
    both = jnp.concatenate([own, swap(own, "core")], axis=1)
    return both[0], both[1]


def return_plane(partial):
    half = partial.shape[0] // 2
    core_sum = partial[:half].astype(jnp.float32) + swap(partial[half:], "core").astype(jnp.float32)
    core_sum = core_sum.astype(jnp.bfloat16).reshape(4, half // 4, -1)
    total = core_sum[0].astype(jnp.float32)
    for k, by in ((1, 3), (2, 1), (3, 2)):
        total = total + shift(core_sum[k], by).astype(jnp.float32)
    return total


def expert_part(x_rows, g_rows, w_in, w_out):
    pre_act = dot_f32(x_rows, w_in, ((1,), (0,)))
    value, slope = gelu_pair(pre_act)
    back_hid = dot_f32(g_rows, w_out, ((1,), (1,)))
    hid_grad = (back_hid * slope).astype(jnp.bfloat16)
    partial = dot_f32(hid_grad, w_in, ((1,), (1,))).astype(jnp.bfloat16)
    return value.astype(jnp.bfloat16), hid_grad, partial


def shards(inputs, out_grad, routes, router_weight, w_in, w_out):
    d_model = inputs.shape[1]
    ff_dev = w_in.shape[1]
    send, sel = slot_rows(inputs, out_grad, routes, router_weight)
    got = lax.all_to_all(send.reshape(4, 2 * CAP, d_model), "x", 0, 0, tiled=True)
    near = got.reshape(4, 2, CAP, d_model).transpose(1, 0, 2, 3).reshape(2, 4 * CAP, d_model)
    far = swap(near, "zh")
    x_near, g_near = gather_plane(near)
    hidden_near, hid_grad_near, partial_near = expert_part(x_near, g_near, w_in, w_out)
    x_far, g_far = gather_plane(far)
    hidden_far, hid_grad_far, partial_far = expert_part(x_far, g_far, w_in, w_out)
    x_all = jnp.concatenate([x_near, x_far], axis=0)
    g_all = jnp.concatenate([g_near, g_far], axis=0)
    hidden = jnp.concatenate([hidden_near, hidden_far], axis=0)
    hid_grad = jnp.concatenate([hid_grad_near, hid_grad_far], axis=0)
    grad_in = dot_f32(x_all, hid_grad, ((0,), (0,))).astype(jnp.bfloat16)
    grad_out = dot_f32(g_all, hidden, ((0,), (0,))).astype(jnp.bfloat16)
    both = lax.psum_scatter(
        jnp.concatenate([grad_in, grad_out], axis=1), "group", scatter_dimension=0, tiled=True
    )
    back_far = return_plane(partial_far).astype(jnp.bfloat16)
    slots = return_plane(partial_near) + swap(back_far, "zh").astype(jnp.float32)
    slots = lax.all_to_all(
        slots.astype(jnp.bfloat16).reshape(4, CAP, d_model), "x", 0, 0, tiled=True
    ).reshape(4 * CAP, d_model)
    n_tok = inputs.shape[0]
    sel_slots = sel.reshape(4, 2, CAP, n_tok)[:, 0].reshape(4 * CAP, n_tok)
    in_grad = dot_f32(sel_slots, slots, ((0,), (0,))).astype(jnp.bfloat16)
    return in_grad, both[:, :ff_dev], both[:, ff_dev:].T


def solution(mesh):
    fine = Mesh(mesh.devices.reshape(SPLIT_AXES), AXES)
    everyone = ("group",) + LOCAL
    return jax.shard_map(
        shards,
        mesh=fine,
        in_specs=(
            P(everyone, None),
            P(everyone, None),
            P(everyone, None),
            P(),
            P(None, LOCAL),
            P(LOCAL, None),
        ),
        out_specs=(P(everyone, None), P("group", LOCAL), P(LOCAL, "group")),
        check_vma=False,
    )
```

```python
import jax
import jax.numpy as jnp
from jax import lax
from jax.sharding import Mesh, PartitionSpec as P

CAP = 4
SPLIT_AXES = (16, 4, 2, 4, 2)
AXES = ("group", "x", "zh", "y", "core")
LOCAL = ("x", "zh", "y", "core")

gelu_c = 0.7978845608
gelu_a = 0.044715


def gelu_pair(pre_act):
    inner = gelu_c * (pre_act + gelu_a * pre_act * pre_act * pre_act)
    tval = jnp.tanh(inner)
    value = 0.5 * pre_act * (1.0 + tval)
    slope = 0.5 * (1.0 + tval) + 0.5 * pre_act * (1.0 - tval * tval) * gelu_c * (
        1.0 + 3.0 * gelu_a * pre_act * pre_act
    )
    return (value, slope)


def dot_f32(a, b, dims):
    return lax.dot_general(a, b, (dims, ((), ())), preferred_element_type=jnp.float32)


def swap(value, axis):
    return lax.ppermute(value, axis, [(0, 1), (1, 0)])


def shift(value, by):
    return lax.ppermute(value, "y", [(i, (i + by) % 4) for i in range(4)])


def slot_rows(inputs, out_grad, routes, router_weight):
    tok_rows = inputs.shape[0]
    n_experts = router_weight.shape[1]
    first, second = routes[:, 0], routes[:, 1]
    expert = lax.broadcasted_iota(jnp.int32, (4, tok_rows), 0)
    mine = (first[None, :] == expert) | (second[None, :] == expert)
    other = jnp.where(mine, first[None, :] + second[None, :] - expert, 0)
    earlier = (
        lax.broadcasted_iota(jnp.int32, (tok_rows, tok_rows), 0)
        < lax.broadcasted_iota(jnp.int32, (tok_rows, tok_rows), 1)
    ).astype(jnp.bfloat16)
    slot_pos = dot_f32(mine.astype(jnp.bfloat16), earlier, ((1,), (0,))).astype(jnp.int32)
    slot_ids = lax.broadcasted_iota(jnp.int32, (4, 2 * CAP, tok_rows), 1) % CAP
    picked = mine[:, None, :] & (slot_pos[:, None, :] == slot_ids)
    sel = picked.reshape(-1, tok_rows)
    other_of = jnp.sum(jnp.where(picked, other[:, None, :], 0), axis=2).reshape(-1)
    sel_bf = sel.astype(jnp.bfloat16)
    x_sel = dot_f32(sel_bf, inputs, ((1,), (0,))).astype(jnp.bfloat16)
    dy_sel = dot_f32(sel_bf, out_grad, ((1,), (0,)))
    logits = dot_f32(x_sel, router_weight, ((1,), (0,)))
    n_rows = sel.shape[0]
    lane = lax.broadcasted_iota(jnp.int32, (n_rows, n_experts), 1)
    row = lax.broadcasted_iota(jnp.int32, (n_rows, n_experts), 0)
    own_logit = jnp.sum(jnp.where(lane == row // (2 * CAP), logits, 0.0), axis=1)
    other_logit = jnp.sum(jnp.where(lane == other_of[:, None], logits, 0.0), axis=1)
    gate = 1.0 / (1.0 + jnp.exp(other_logit - own_logit))
    g_sel = (gate[:, None] * dy_sel).astype(jnp.bfloat16)
    is_x = (lax.broadcasted_iota(jnp.int32, (n_rows, 1), 0) // CAP) % 2 == 0
    return jnp.where(is_x, x_sel, g_sel), sel_bf


def kinds_apart(rows):
    n_rows = rows.shape[0]
    to = lax.broadcasted_iota(jnp.int32, (n_rows, n_rows), 0)
    at = lax.broadcasted_iota(jnp.int32, (n_rows, n_rows), 1)
    half = n_rows // 2
    source = (to % half) // CAP * (2 * CAP) + to // half * CAP + to % CAP
    return dot_f32((at == source).astype(jnp.bfloat16), rows, ((1,), (0,))).astype(jnp.bfloat16)


def gather_plane(rows):
    pieces = [rows, shift(rows, 3), shift(rows, 2), shift(rows, 1)]
    across = swap(jnp.concatenate(pieces, axis=0), "core")
    half = rows.shape[0] // 2
    pieces += [across[k * 2 * half : (k + 1) * 2 * half] for k in range(4)]
    return (
        jnp.concatenate([p[:half] for p in pieces], axis=0),
        jnp.concatenate([p[half:] for p in pieces], axis=0),
    )


def expert_part(x_rows, g_rows, w_in, w_out):
    pre_act = dot_f32(x_rows, w_in, ((1,), (0,)))
    value, slope = gelu_pair(pre_act)
    back_hid = dot_f32(g_rows, w_out, ((1,), (1,)))
    return value.astype(jnp.bfloat16), (back_hid * slope).astype(jnp.bfloat16)


def row_order(n_rows):
    to = lax.broadcasted_iota(jnp.int32, (n_rows, n_rows), 0)
    at = lax.broadcasted_iota(jnp.int32, (n_rows, n_rows), 1)
    y = (to // 64 - lax.axis_index("y")) & 3
    core = (to // 32 - lax.axis_index("core")) & 1
    zh = (to // 16 - lax.axis_index("zh")) & 1
    return (at == zh * 128 + core * 64 + y * 16 + (to & 15)).astype(jnp.bfloat16)


def flip_cores(rows):
    n_rows, width = rows.shape
    parts = rows.reshape(2, 2, n_rows // 4, width)
    return jnp.concatenate([parts[:, 1:], parts[:, :1]], axis=1).reshape(n_rows, width)


def columns(rows, begin, width):
    return lax.dynamic_slice(
        rows, (0, begin), (rows.shape[0], width), allow_negative_indices=False
    )


def line_sums(streams, n_group):
    width = streams[0][0].shape[1] // n_group
    top = (n_group - 1) * width
    here = lax.axis_index("group") * width
    towards = width * (1 - 2 * lax.axis_index("core"))
    carried = [None] * len(streams)
    for step in range(n_group - 1):
        ahead = n_group - 1 - step
        begin = lax.clamp(0, here + ahead * towards, top)
        pairs = [(2 * i, 2 * i + 2) for i in range(step + 1)]
        pairs += [(2 * n_group - 1 - 2 * i, 2 * n_group - 3 - 2 * i) for i in range(step + 1)]
        for k, (rows, units) in enumerate(streams):
            cut = columns(rows, begin, width)
            term = dot_f32(cut, units, ((0,), (0,)))
            if carried[k] is not None:
                term = term + carried[k].astype(jnp.float32)
            carried[k] = lax.ppermute(term.astype(jnp.bfloat16), ("group", "core"), pairs)
    return carried


def shards(inputs, out_grad, routes, router_weight, w_in, w_out):
    n_tok, d_model = inputs.shape
    ff_dev = w_in.shape[1]
    n_group = lax.axis_size("group")
    send, sel = slot_rows(inputs, out_grad, routes, router_weight)
    got = lax.all_to_all(send.reshape(4, 2 * CAP, d_model), "x", 0, 0, tiled=True)
    near = kinds_apart(got.reshape(8 * CAP, d_model))
    far, order = lax.optimization_barrier((swap(near, "zh"), row_order(64 * CAP)))
    x_near, g_near = gather_plane(near)
    hidden_near, hid_grad_near = expert_part(x_near, g_near, w_in, w_out)
    x_far, g_far = gather_plane(far)
    hidden_far, hid_grad_far = expert_part(x_far, g_far, w_in, w_out)
    x_all = jnp.concatenate([x_near, x_far], axis=0)
    g_all = jnp.concatenate([g_near, g_far], axis=0)
    hidden = jnp.concatenate([hidden_near, hidden_far], axis=0)
    hid_grad = jnp.concatenate([hid_grad_near, hid_grad_far], axis=0)
    other = flip_cores(swap(jnp.concatenate([hid_grad, hidden], axis=1), "core"))
    hid_grad_both = jnp.concatenate([hid_grad, other[:, :ff_dev]], axis=1)
    hidden_both = jnp.concatenate([hidden, other[:, ff_dev:]], axis=1)

    ordered = dot_f32(order, hid_grad, ((1,), (0,))).astype(jnp.bfloat16)
    partial = dot_f32(ordered, w_in, ((1,), (1,))).astype(jnp.bfloat16)
    hid_grad_both, partial = lax.optimization_barrier((hid_grad_both, partial))
    plane = lax.psum_scatter(partial, ("y", "core"), scatter_dimension=0, tiled=True)
    slots = lax.psum_scatter(plane, "zh", scatter_dimension=0, tiled=True)
    slots = lax.all_to_all(slots.reshape(4, CAP, d_model), "x", 0, 0, tiled=True)
    slots = slots.reshape(4 * CAP, d_model)
    sel_slots = sel.reshape(4, 2, CAP, n_tok)[:, 0].reshape(4 * CAP, n_tok)
    in_grad = dot_f32(sel_slots, slots, ((0,), (0,))).astype(jnp.bfloat16)

    sum_in, sum_out = line_sums([(x_all, hid_grad_both), (g_all, hidden_both)], n_group)
    width = d_model // n_group
    here = lax.axis_index("group") * width
    own_in = dot_f32(columns(x_all, here, width), hid_grad, ((0,), (0,)))
    own_out = dot_f32(hidden, columns(g_all, here, width), ((0,), (0,)))
    across = swap(jnp.concatenate([sum_in[:, ff_dev:], sum_out[:, ff_dev:]], axis=1), "core")
    across = across.astype(jnp.float32)
    w_in_grad = own_in + sum_in[:, :ff_dev].astype(jnp.float32) + across[:, :ff_dev]
    sum_out = sum_out[:, :ff_dev].astype(jnp.float32) + across[:, ff_dev:]
    w_out_grad = own_out + sum_out.T
    return in_grad, w_in_grad.astype(jnp.bfloat16), w_out_grad.astype(jnp.bfloat16)


def solution(mesh):
    fine = Mesh(mesh.devices.reshape(SPLIT_AXES), AXES)
    everyone = ("group",) + LOCAL
    return jax.shard_map(
        shards,
        mesh=fine,
        in_specs=(
            P(everyone, None),
            P(everyone, None),
            P(everyone, None),
            P(),
            P(None, LOCAL),
            P(LOCAL, None),
        ),
        out_specs=(P(everyone, None), P("group", LOCAL), P(LOCAL, "group")),
        check_vma=False,
    )
```

```python
import jax
import jax.numpy as jnp
from jax import lax
from jax.sharding import Mesh, PartitionSpec as P

CAP = 4
SPLIT_AXES = (16, 4, 2, 4, 2)
AXES = ("group", "x", "zh", "y", "core")
LOCAL = ("x", "zh", "y", "core")

gelu_c = 0.7978845608
gelu_a = 0.044715


def gelu_pair(pre_act):
    inner = gelu_c * (pre_act + gelu_a * pre_act * pre_act * pre_act)
    tval = jnp.tanh(inner)
    value = 0.5 * pre_act * (1.0 + tval)
    slope = 0.5 * (1.0 + tval) + 0.5 * pre_act * (1.0 - tval * tval) * gelu_c * (
        1.0 + 3.0 * gelu_a * pre_act * pre_act
    )
    return (value, slope)


def dot_f32(a, b, dims):
    return lax.dot_general(a, b, (dims, ((), ())), preferred_element_type=jnp.float32)


def swap(value, axis):
    return lax.ppermute(value, axis, [(0, 1), (1, 0)])


def shift(value, by):
    return lax.ppermute(value, "y", [(i, (i + by) % 4) for i in range(4)])


def slot_rows(inputs, out_grad, routes, router_weight):
    tok_rows = inputs.shape[0]
    n_experts = router_weight.shape[1]
    first, second = routes[:, 0], routes[:, 1]
    expert = lax.broadcasted_iota(jnp.int32, (4, tok_rows), 0)
    mine = (first[None, :] == expert) | (second[None, :] == expert)
    other = jnp.where(mine, first[None, :] + second[None, :] - expert, 0)
    earlier = (
        lax.broadcasted_iota(jnp.int32, (tok_rows, tok_rows), 0)
        < lax.broadcasted_iota(jnp.int32, (tok_rows, tok_rows), 1)
    ).astype(jnp.bfloat16)
    slot_pos = dot_f32(mine.astype(jnp.bfloat16), earlier, ((1,), (0,))).astype(jnp.int32)
    slot_ids = lax.broadcasted_iota(jnp.int32, (4, 2 * CAP, tok_rows), 1) % CAP
    picked = mine[:, None, :] & (slot_pos[:, None, :] == slot_ids)
    sel = picked.reshape(-1, tok_rows)
    other_of = jnp.sum(jnp.where(picked, other[:, None, :], 0), axis=2).reshape(-1)
    sel_bf = sel.astype(jnp.bfloat16)
    x_sel = dot_f32(sel_bf, inputs, ((1,), (0,))).astype(jnp.bfloat16)
    dy_sel = dot_f32(sel_bf, out_grad, ((1,), (0,)))
    logits = dot_f32(x_sel, router_weight, ((1,), (0,)))
    n_rows = sel.shape[0]
    lane = lax.broadcasted_iota(jnp.int32, (n_rows, n_experts), 1)
    row = lax.broadcasted_iota(jnp.int32, (n_rows, n_experts), 0)
    own_logit = jnp.sum(jnp.where(lane == row // (2 * CAP), logits, 0.0), axis=1)
    other_logit = jnp.sum(jnp.where(lane == other_of[:, None], logits, 0.0), axis=1)
    gate = 1.0 / (1.0 + jnp.exp(other_logit - own_logit))
    g_sel = (gate[:, None] * dy_sel).astype(jnp.bfloat16)
    is_x = (lax.broadcasted_iota(jnp.int32, (n_rows, 1), 0) // CAP) % 2 == 0
    return jnp.where(is_x, x_sel, g_sel), sel_bf


def gather_plane(rows):
    pieces = [rows, shift(rows, 3), shift(rows, 2), shift(rows, 1)]
    own = jnp.concatenate(pieces, axis=0)
    return jnp.concatenate([own, swap(own, "core")], axis=0)


def row_order(n_rows, kind):
    to = lax.broadcasted_iota(jnp.int32, (n_rows, 2 * n_rows), 0)
    at = lax.broadcasted_iota(jnp.int32, (n_rows, 2 * n_rows), 1)
    core = (to // 128 - lax.axis_index("core")) & 1
    source = core * 256 + ((to & 127) // CAP) * (2 * CAP) + kind * CAP + (to & (CAP - 1))
    return (at == source).astype(jnp.bfloat16)


def expert_part(x_rows, g_rows, w_in, w_out):
    pre_act = dot_f32(x_rows, w_in, ((1,), (0,)))
    value, slope = gelu_pair(pre_act)
    back_hid = dot_f32(g_rows, w_out, ((1,), (1,)))
    return value.astype(jnp.bfloat16), (back_hid * slope).astype(jnp.bfloat16)


def block_of(rows, begin, height):
    return lax.dynamic_slice(
        rows, (begin, 0), (height, rows.shape[1]), allow_negative_indices=False
    )


def line_sums(streams, n_group, beside, ties):
    height = streams[0].shape[0] // n_group
    top = (n_group - 1) * height
    here, core = lax.axis_index("group"), lax.axis_index("core")
    rank = jnp.where(core == 0, here, n_group - 1 - here)
    towards = height * (1 - 2 * core)
    pairs = [(2 * i, 2 * i + 2) for i in range(n_group - 1)]
    pairs += [(2 * i + 3, 2 * i + 1) for i in range(n_group - 1)]
    carried = [None] * len(streams)
    for step in range(n_group - 1):
        begin = lax.clamp(0, here * height + (n_group - 1 - step) * towards, top)
        for k, rows in enumerate(streams):
            term = block_of(rows, begin, height)
            if step:
                arrived = jnp.where(rank <= step, carried[k].astype(jnp.float32), 0.0)
                term = (term.astype(jnp.float32) + arrived).astype(jnp.bfloat16)
            carried[k] = lax.ppermute(term, ("group", "core"), pairs)
        if step in ties:
            beside, carried[0] = lax.optimization_barrier((beside, carried[0]))
            beside = ties[step](beside)
    return carried, beside


def shards(inputs, out_grad, routes, router_weight, w_in, w_out):
    n_tok, d_model = inputs.shape
    ff_dev = w_in.shape[1]
    n_group = lax.axis_size("group")
    send, sel = slot_rows(inputs, out_grad, routes, router_weight)
    got = lax.all_to_all(send.reshape(4, 2 * CAP, d_model), "x", 0, 0, tiled=True)
    got = got.reshape(8 * CAP, d_model)
    far, order_x, order_g = lax.optimization_barrier(
        (swap(got, "zh"), row_order(64 * CAP, 0), row_order(64 * CAP, 1))
    )
    rows = gather_plane(jnp.concatenate([got, far], axis=0))
    x_all = dot_f32(order_x, rows, ((1,), (0,))).astype(jnp.bfloat16)
    g_all = dot_f32(order_g, rows, ((1,), (0,))).astype(jnp.bfloat16)
    hidden, hid_grad = expert_part(x_all, g_all, w_in, w_out)
    other = swap(jnp.concatenate([hid_grad, hidden], axis=1), "core")
    partial = dot_f32(hid_grad, w_in, ((1,), (1,))).astype(jnp.bfloat16)
    hid_grad_both = jnp.concatenate([hid_grad, other[:, :ff_dev]], axis=1)
    hidden_both = jnp.concatenate([hidden, other[:, ff_dev:]], axis=1)
    hid_grad_both, partial = lax.optimization_barrier((hid_grad_both, partial))
    grad_in = dot_f32(x_all, hid_grad_both, ((0,), (0,))).astype(jnp.bfloat16)
    grad_out = dot_f32(g_all, hidden_both, ((0,), (0,))).astype(jnp.bfloat16)

    def along_y(rows):
        parts = rows.reshape(4, -1, d_model)
        total = parts[0].astype(jnp.float32)
        for by in (1, 3, 2):
            total = total + shift(parts[by], by).astype(jnp.float32)
        return total.astype(jnp.bfloat16)

    def across_zh(rows):
        half = rows.shape[0] // 2
        total = rows[:half].astype(jnp.float32) + swap(rows[half:], "zh").astype(jnp.float32)
        return total.astype(jnp.bfloat16)

    def along_x(rows):
        parts = rows.reshape(4, CAP, d_model)
        return lax.all_to_all(parts, "x", 0, 0, tiled=True).reshape(4 * CAP, d_model)

    core, half = lax.axis_index("core"), partial.shape[0] // 2
    given = swap(block_of(partial, (1 - core) * half, half), "core").astype(jnp.float32)
    given = (block_of(partial, core * half, half).astype(jnp.float32) + given).astype(jnp.bfloat16)
    (sum_in, sum_out), slots = line_sums(
        [grad_in, grad_out], n_group, given, {0: along_y, 3: across_zh, 9: along_x}
    )
    sel_slots = sel.reshape(4, 2, CAP, n_tok)[:, 0].reshape(4 * CAP, n_tok)
    in_grad = dot_f32(sel_slots, slots, ((0,), (0,))).astype(jnp.bfloat16)

    width = d_model // n_group
    here = lax.axis_index("group") * width
    own_in = block_of(grad_in, here, width)[:, :ff_dev].astype(jnp.float32)
    own_out = block_of(grad_out, here, width)[:, :ff_dev].astype(jnp.float32)
    across = swap(jnp.concatenate([sum_in[:, ff_dev:], sum_out[:, ff_dev:]], axis=1), "core")
    across = across.astype(jnp.float32)
    w_in_grad = own_in + sum_in[:, :ff_dev].astype(jnp.float32) + across[:, :ff_dev]
    w_out_grad = own_out + sum_out[:, :ff_dev].astype(jnp.float32) + across[:, ff_dev:]
    return in_grad, w_in_grad.astype(jnp.bfloat16), w_out_grad.astype(jnp.bfloat16).T


def solution(mesh):
    fine = Mesh(mesh.devices.reshape(SPLIT_AXES), AXES)
    everyone = ("group",) + LOCAL
    return jax.shard_map(
        shards,
        mesh=fine,
        in_specs=(
            P(everyone, None),
            P(everyone, None),
            P(everyone, None),
            P(),
            P(None, LOCAL),
            P(LOCAL, None),
        ),
        out_specs=(P(everyone, None), P("group", LOCAL), P(LOCAL, "group")),
        check_vma=False,
    )
```

```python
import jax
import jax.numpy as jnp
from jax import lax
from jax.sharding import Mesh, PartitionSpec as P

CAP = 4
SPLIT_AXES = (16, 4, 2, 4, 2)
AXES = ("group", "x", "zh", "y", "core")
LOCAL = ("x", "zh", "y", "core")

gelu_c = 0.7978845608
gelu_a = 0.044715


def gelu_pair(pre_act):
    inner = gelu_c * (pre_act + gelu_a * pre_act * pre_act * pre_act)
    tval = jnp.tanh(inner)
    value = 0.5 * pre_act * (1.0 + tval)
    slope = 0.5 * (1.0 + tval) + 0.5 * pre_act * (1.0 - tval * tval) * gelu_c * (
        1.0 + 3.0 * gelu_a * pre_act * pre_act
    )
    return (value, slope)


def dot_f32(a, b, dims):
    return lax.dot_general(a, b, (dims, ((), ())), preferred_element_type=jnp.float32)


def swap(value, axis):
    return lax.ppermute(value, axis, [(0, 1), (1, 0)])


def shift(value, by):
    return lax.ppermute(value, "y", [(i, (i + by) % 4) for i in range(4)])


def slot_rows(inputs, out_grad, routes, router_weight):
    tok_rows = inputs.shape[0]
    n_experts = router_weight.shape[1]
    first, second = routes[:, 0], routes[:, 1]
    expert = lax.broadcasted_iota(jnp.int32, (4, tok_rows), 0)
    mine = (first[None, :] == expert) | (second[None, :] == expert)
    other = jnp.where(mine, first[None, :] + second[None, :] - expert, 0)
    earlier = (
        lax.broadcasted_iota(jnp.int32, (tok_rows, tok_rows), 0)
        < lax.broadcasted_iota(jnp.int32, (tok_rows, tok_rows), 1)
    ).astype(jnp.bfloat16)
    slot_pos = dot_f32(mine.astype(jnp.bfloat16), earlier, ((1,), (0,))).astype(jnp.int32)
    slot_ids = lax.broadcasted_iota(jnp.int32, (4, 2 * CAP, tok_rows), 1) % CAP
    picked = mine[:, None, :] & (slot_pos[:, None, :] == slot_ids)
    sel = picked.reshape(-1, tok_rows)
    other_of = jnp.sum(jnp.where(picked, other[:, None, :], 0), axis=2).reshape(-1)
    sel_bf = sel.astype(jnp.bfloat16)
    x_sel = dot_f32(sel_bf, inputs, ((1,), (0,))).astype(jnp.bfloat16)
    dy_sel = dot_f32(sel_bf, out_grad, ((1,), (0,)))
    logits = dot_f32(x_sel, router_weight, ((1,), (0,)))
    n_rows = sel.shape[0]
    lane = lax.broadcasted_iota(jnp.int32, (n_rows, n_experts), 1)
    row = lax.broadcasted_iota(jnp.int32, (n_rows, n_experts), 0)
    own_logit = jnp.sum(jnp.where(lane == row // (2 * CAP), logits, 0.0), axis=1)
    other_logit = jnp.sum(jnp.where(lane == other_of[:, None], logits, 0.0), axis=1)
    gate = 1.0 / (1.0 + jnp.exp(other_logit - own_logit))
    g_sel = (gate[:, None] * dy_sel).astype(jnp.bfloat16)
    is_x = (lax.broadcasted_iota(jnp.int32, (n_rows, 1), 0) // CAP) % 2 == 0
    return jnp.where(is_x, x_sel, g_sel), sel_bf


def gather_plane(rows):
    pieces = [rows, shift(rows, 3), shift(rows, 2), shift(rows, 1)]
    own = jnp.concatenate(pieces, axis=0)
    return jnp.concatenate([own, swap(own, "core")], axis=0)


def row_order(n_rows, kind):
    to = lax.broadcasted_iota(jnp.int32, (n_rows, 2 * n_rows), 0)
    at = lax.broadcasted_iota(jnp.int32, (n_rows, 2 * n_rows), 1)
    core = (to // 128 - lax.axis_index("core")) & 1
    source = core * 256 + ((to & 127) // CAP) * (2 * CAP) + kind * CAP + (to & (CAP - 1))
    return (at == source).astype(jnp.bfloat16)


def expert_part(x_rows, g_rows, w_in, w_out):
    pre_act = dot_f32(x_rows, w_in, ((1,), (0,)))
    value, slope = gelu_pair(pre_act)
    back_hid = dot_f32(g_rows, w_out, ((1,), (1,)))
    return value.astype(jnp.bfloat16), (back_hid * slope).astype(jnp.bfloat16)


def block_of(rows, begin, height):
    return lax.dynamic_slice(
        rows, (begin, 0), (height, rows.shape[1]), allow_negative_indices=False
    )


def line_sums(streams, n_group, beside, ties):
    height = streams[0].shape[0] // n_group
    top = (n_group - 1) * height
    here, core = lax.axis_index("group"), lax.axis_index("core")
    rank = jnp.where(core == 0, here, n_group - 1 - here)
    towards = height * (1 - 2 * core)
    pairs = [(2 * i, 2 * i + 2) for i in range(n_group - 1)]
    pairs += [(2 * i + 3, 2 * i + 1) for i in range(n_group - 1)]
    carried, last = [None] * len(streams), streams[0]
    for step in range(n_group - 1):
        begin = lax.clamp(0, here * height + (n_group - 1 - step) * towards, top)
        for k, rows in enumerate(streams):
            term = block_of(rows, begin, height)
            if step:
                carried[k], last = lax.optimization_barrier((carried[k], last))
                term = term + jnp.where(rank <= step, carried[k], jnp.zeros_like(carried[k]))
            carried[k], last = lax.ppermute(term, ("group", "core"), pairs), term
        if step in ties:
            beside, carried[0] = lax.optimization_barrier((beside, carried[0]))
            beside = ties[step](beside)
    return carried, beside


def shards(inputs, out_grad, routes, router_weight, w_in, w_out):
    n_tok, d_model = inputs.shape
    ff_dev = w_in.shape[1]
    n_group = lax.axis_size("group")
    send, sel = slot_rows(inputs, out_grad, routes, router_weight)
    got = lax.all_to_all(send.reshape(4, 2 * CAP, d_model), "x", 0, 0, tiled=True)
    got = got.reshape(8 * CAP, d_model)
    far, order_x, order_g = lax.optimization_barrier(
        (swap(got, "zh"), row_order(64 * CAP, 0), row_order(64 * CAP, 1))
    )
    rows = gather_plane(jnp.concatenate([got, far], axis=0))
    x_all = dot_f32(order_x, rows, ((1,), (0,))).astype(jnp.bfloat16)
    g_all = dot_f32(order_g, rows, ((1,), (0,))).astype(jnp.bfloat16)
    hidden, hid_grad = expert_part(x_all, g_all, w_in, w_out)
    other = swap(jnp.concatenate([hid_grad, hidden], axis=1), "core")
    partial = dot_f32(hid_grad, w_in, ((1,), (1,))).astype(jnp.bfloat16)

    def product(rows, units):
        return dot_f32(rows, units, ((0,), (0,))).astype(jnp.bfloat16)

    cut = ff_dev // 2
    own_in = product(x_all, hid_grad)
    own_out = product(g_all, hidden)
    other_in = product(x_all, other[:, :ff_dev])
    other_out = product(g_all, other[:, ff_dev:])
    streams = [
        own_in,
        jnp.concatenate([own_out, other_in[:, :cut]], axis=1),
        jnp.concatenate([other_in[:, cut:], other_out], axis=1),
    ]

    def along_y(rows):
        parts = rows.reshape(4, -1, d_model)
        total = parts[0].astype(jnp.float32)
        for by in (1, 3, 2):
            total = total + shift(parts[by], by).astype(jnp.float32)
        total = total.astype(jnp.bfloat16)
        turned = jnp.concatenate([total[4 * CAP :], total[: 4 * CAP]], axis=0)
        return jnp.where(lax.axis_index("zh") == 0, total, turned)

    def across_zh(rows):
        return lax.psum_scatter(rows, "zh", scatter_dimension=0, tiled=True)

    def along_x(rows):
        parts = rows.reshape(4, CAP, d_model)
        return lax.all_to_all(parts, "x", 0, 0, tiled=True).reshape(4 * CAP, d_model)

    core, half = lax.axis_index("core"), partial.shape[0] // 2
    given = swap(block_of(partial, (1 - core) * half, half), "core").astype(jnp.float32)
    given = (block_of(partial, core * half, half).astype(jnp.float32) + given).astype(jnp.bfloat16)
    sel_slots = sel.reshape(4, 2, CAP, n_tok)[:, 0].reshape(4 * CAP, n_tok)

    def to_tokens(rows):
        return dot_f32(sel_slots, rows, ((0,), (0,))).astype(jnp.bfloat16)

    sums, in_grad = line_sums(
        streams, n_group, given, {0: along_y, 3: across_zh, 11: along_x, 14: to_tokens}
    )
    width = d_model // n_group
    here = lax.axis_index("group") * width
    across = swap(jnp.concatenate([sums[1][:, ff_dev:], sums[2]], axis=1), "core")

    def total(own, carried, given):
        parts = (block_of(own, here, width), carried, given)
        return sum(part.astype(jnp.float32) for part in parts).astype(jnp.bfloat16)

    w_in_grad = total(own_in, sums[0], across[:, :ff_dev])
    w_out_grad = total(own_out, sums[1][:, :ff_dev], across[:, ff_dev:])
    return in_grad, w_in_grad, w_out_grad.T


def solution(mesh):
    fine = Mesh(mesh.devices.reshape(SPLIT_AXES), AXES)
    everyone = ("group",) + LOCAL
    return jax.shard_map(
        shards,
        mesh=fine,
        in_specs=(
            P(everyone, None),
            P(everyone, None),
            P(everyone, None),
            P(),
            P(None, LOCAL),
            P(LOCAL, None),
        ),
        out_specs=(P(everyone, None), P("group", LOCAL), P(LOCAL, "group")),
        check_vma=False,
    )
```

```python
import jax
import jax.numpy as jnp
from jax import lax
from jax.sharding import Mesh, PartitionSpec as P

CAP = 4
SPLIT_AXES = (16, 4, 2, 4, 2)
AXES = ("group", "x", "zh", "y", "core")
LOCAL = ("x", "zh", "y", "core")

gelu_c = 0.7978845608
gelu_a = 0.044715


def gelu_pair(pre_act):
    inner = gelu_c * (pre_act + gelu_a * pre_act * pre_act * pre_act)
    tval = jnp.tanh(inner)
    value = 0.5 * pre_act * (1.0 + tval)
    slope = 0.5 * (1.0 + tval) + 0.5 * pre_act * (1.0 - tval * tval) * gelu_c * (
        1.0 + 3.0 * gelu_a * pre_act * pre_act
    )
    return (value, slope)


def dot_f32(a, b, dims):
    return lax.dot_general(a, b, (dims, ((), ())), preferred_element_type=jnp.float32)


def swap(value, axis):
    return lax.ppermute(value, axis, [(0, 1), (1, 0)])


def shift(value, by):
    return lax.ppermute(value, "y", [(i, (i + by) % 4) for i in range(4)])


def slot_rows(inputs, out_grad, routes, router_weight):
    tok_rows = inputs.shape[0]
    n_experts = router_weight.shape[1]
    first, second = routes[:, 0], routes[:, 1]
    expert = lax.broadcasted_iota(jnp.int32, (4, tok_rows), 0)
    mine = (first[None, :] == expert) | (second[None, :] == expert)
    other = jnp.where(mine, first[None, :] + second[None, :] - expert, 0)
    earlier = (
        lax.broadcasted_iota(jnp.int32, (tok_rows, tok_rows), 0)
        < lax.broadcasted_iota(jnp.int32, (tok_rows, tok_rows), 1)
    ).astype(jnp.bfloat16)
    slot_pos = dot_f32(mine.astype(jnp.bfloat16), earlier, ((1,), (0,))).astype(jnp.int32)
    slot_ids = lax.broadcasted_iota(jnp.int32, (4, 2 * CAP, tok_rows), 1) % CAP
    picked = mine[:, None, :] & (slot_pos[:, None, :] == slot_ids)
    sel = picked.reshape(-1, tok_rows)
    other_of = jnp.sum(jnp.where(picked, other[:, None, :], 0), axis=2).reshape(-1)
    sel_bf = sel.astype(jnp.bfloat16)
    x_sel = dot_f32(sel_bf, inputs, ((1,), (0,))).astype(jnp.bfloat16)
    dy_sel = dot_f32(sel_bf, out_grad, ((1,), (0,)))
    logits = dot_f32(x_sel, router_weight, ((1,), (0,)))
    n_rows = sel.shape[0]
    lane = lax.broadcasted_iota(jnp.int32, (n_rows, n_experts), 1)
    row = lax.broadcasted_iota(jnp.int32, (n_rows, n_experts), 0)
    own_logit = jnp.sum(jnp.where(lane == row // (2 * CAP), logits, 0.0), axis=1)
    other_logit = jnp.sum(jnp.where(lane == other_of[:, None], logits, 0.0), axis=1)
    gate = 1.0 / (1.0 + jnp.exp(other_logit - own_logit))
    g_sel = (gate[:, None] * dy_sel).astype(jnp.bfloat16)
    is_x = (lax.broadcasted_iota(jnp.int32, (n_rows, 1), 0) // CAP) % 2 == 0
    return jnp.where(is_x, x_sel, g_sel), sel_bf


def gather_plane(rows):
    pieces = [rows, shift(rows, 3), shift(rows, 2), shift(rows, 1)]
    own = jnp.concatenate(pieces, axis=0)
    return own, swap(own, "core")


def row_order(n_rows, kind):
    to = lax.broadcasted_iota(jnp.int32, (n_rows, 2 * n_rows), 0)
    at = lax.broadcasted_iota(jnp.int32, (n_rows, 2 * n_rows), 1)
    core = (to // 128 - lax.axis_index("core")) & 1
    source = core * 256 + ((to & 127) // CAP) * (2 * CAP) + kind * CAP + (to & (CAP - 1))
    return (at == source).astype(jnp.bfloat16)


def home_order(n_rows):
    to = lax.broadcasted_iota(jnp.int32, (n_rows, n_rows), 0)
    at = lax.broadcasted_iota(jnp.int32, (n_rows, n_rows), 1)
    zh = (to // CAP - lax.axis_index("zh")) & 1
    source = zh * 16 + to // (2 * CAP) * CAP + (to & (CAP - 1))
    return (at == source).astype(jnp.bfloat16)


def block_of(rows, begin, height):
    return lax.dynamic_slice(
        rows, (begin, 0), (height, rows.shape[1]), allow_negative_indices=False
    )


def line_sums(streams, n_group, beside, ties):
    height = streams[0].shape[0] // n_group
    top = (n_group - 1) * height
    here, core = lax.axis_index("group"), lax.axis_index("core")
    rank = jnp.where(core == 0, here, n_group - 1 - here)
    towards = height * (1 - 2 * core)
    pairs = [(2 * i, 2 * i + 2) for i in range(n_group - 1)]
    pairs += [(2 * i + 3, 2 * i + 1) for i in range(n_group - 1)]
    carried, last = [None] * len(streams), streams[0]
    for step in range(n_group - 1):
        begin = lax.clamp(0, here * height + (n_group - 1 - step) * towards, top)
        for k, rows in enumerate(streams):
            term = block_of(rows, begin, height)
            if step:
                carried[k], last = lax.optimization_barrier((carried[k], last))
                term = term + jnp.where(rank <= step, carried[k], jnp.zeros_like(carried[k]))
            carried[k], last = lax.ppermute(term, ("group", "core"), pairs), term
        if step in ties:
            beside, carried[0] = lax.optimization_barrier((beside, carried[0]))
            beside = ties[step](beside)
    return carried, beside


def shards(inputs, out_grad, routes, router_weight, w_in, w_out):
    n_tok, d_model = inputs.shape
    ff_dev = w_in.shape[1]
    n_group = lax.axis_size("group")
    send, sel = slot_rows(inputs, out_grad, routes, router_weight)
    got = lax.all_to_all(send.reshape(4, 2 * CAP, d_model), "x", 0, 0, tiled=True)
    got = got.reshape(8 * CAP, d_model)
    far, order_x, order_g = lax.optimization_barrier(
        (swap(got, "zh"), row_order(64 * CAP, 0), row_order(64 * CAP, 1))
    )
    own, across = gather_plane(jnp.concatenate([got, far], axis=0))

    def in_order(order):
        half = order.shape[1] // 2
        total = dot_f32(order[:, :half], own, ((1,), (0,)))
        return (total + dot_f32(order[:, half:], across, ((1,), (0,)))).astype(jnp.bfloat16)

    x_all, g_all = in_order(order_x), in_order(order_g)
    pre_act = dot_f32(x_all, w_in, ((1,), (0,)))
    value, slope = gelu_pair(pre_act)
    hidden = value.astype(jnp.bfloat16)
    hidden_both = jnp.concatenate([hidden, swap(hidden, "core")], axis=1)
    back_hid = dot_f32(g_all, w_out, ((1,), (1,)))
    hid_grad = (back_hid * slope).astype(jnp.bfloat16)
    partial = dot_f32(hid_grad, w_in, ((1,), (1,))).astype(jnp.bfloat16)

    def product(rows, units):
        return dot_f32(rows, units, ((0,), (0,))).astype(jnp.bfloat16)

    hid_grad_both = jnp.concatenate([hid_grad, swap(hid_grad, "core")], axis=1)
    grad_out = product(g_all, hidden_both)
    grad_in = product(x_all, hid_grad_both)

    def along_y(rows):
        parts = rows.reshape(4, -1, d_model)
        total = parts[0].astype(jnp.float32)
        for by in (1, 3, 2):
            total = total + shift(parts[by], by).astype(jnp.float32)
        return total.astype(jnp.bfloat16)

    def home(rows):
        parts = dot_f32(home_order(rows.shape[0]), rows, ((1,), (0,))).astype(jnp.bfloat16)
        parts = parts.reshape(8, CAP, d_model)
        return lax.all_to_all(parts, ("x", "zh"), 0, 0, tiled=True).reshape(8 * CAP, d_model)

    core, half = lax.axis_index("core"), partial.shape[0] // 2
    given = swap(block_of(partial, (1 - core) * half, half), "core").astype(jnp.float32)
    given = (block_of(partial, core * half, half).astype(jnp.float32) + given).astype(jnp.bfloat16)
    sums, slots = line_sums(
        [grad_out, grad_in], n_group, given, {0: along_y, 3: lambda rows: rows, 11: home}
    )
    in_grad = dot_f32(sel, slots, ((0,), (0,))).astype(jnp.bfloat16)
    width = d_model // n_group
    here = lax.axis_index("group") * width
    across = [swap(carried[:, ff_dev:], "core") for carried in sums]

    def total(own, carried, given):
        parts = (block_of(own, here, width)[:, :ff_dev], carried[:, :ff_dev], given)
        return sum(part.astype(jnp.float32) for part in parts).astype(jnp.bfloat16)

    w_out_grad = total(grad_out, sums[0], across[0])
    w_in_grad = total(grad_in, sums[1], across[1])
    return in_grad, w_in_grad, w_out_grad.T


def solution(mesh):
    fine = Mesh(mesh.devices.reshape(SPLIT_AXES), AXES)
    everyone = ("group",) + LOCAL
    return jax.shard_map(
        shards,
        mesh=fine,
        in_specs=(
            P(everyone, None),
            P(everyone, None),
            P(everyone, None),
            P(),
            P(None, LOCAL),
            P(LOCAL, None),
        ),
        out_specs=(P(everyone, None), P("group", LOCAL), P(LOCAL, "group")),
        check_vma=False,
    )
```

```python
import jax
import jax.numpy as jnp
from jax import lax
from jax.sharding import Mesh, PartitionSpec as P

CAP = 4
SPLIT_AXES = (16, 4, 2, 4, 2)
AXES = ("group", "x", "zh", "y", "core")
LOCAL = ("x", "zh", "y", "core")

gelu_c = 0.7978845608
gelu_a = 0.044715


def gelu_pair(pre_act):
    inner = gelu_c * (pre_act + gelu_a * pre_act * pre_act * pre_act)
    tval = jnp.tanh(inner)
    value = 0.5 * pre_act * (1.0 + tval)
    slope = 0.5 * (1.0 + tval) + 0.5 * pre_act * (1.0 - tval * tval) * gelu_c * (
        1.0 + 3.0 * gelu_a * pre_act * pre_act
    )
    return (value, slope)


def dot_f32(a, b, dims):
    return lax.dot_general(a, b, (dims, ((), ())), preferred_element_type=jnp.float32)


def swap(value, axis):
    return lax.ppermute(value, axis, [(0, 1), (1, 0)])


def shift(value, by):
    return lax.ppermute(value, "y", [(i, (i + by) % 4) for i in range(4)])


def slot_rows(inputs, out_grad, routes, router_weight):
    tok_rows = inputs.shape[0]
    n_experts = router_weight.shape[1]
    first, second = routes[:, 0], routes[:, 1]
    expert = lax.broadcasted_iota(jnp.int32, (4, tok_rows), 0)
    mine = (first[None, :] == expert) | (second[None, :] == expert)
    other = jnp.where(mine, first[None, :] + second[None, :] - expert, 0)
    earlier = (
        lax.broadcasted_iota(jnp.int32, (tok_rows, tok_rows), 0)
        < lax.broadcasted_iota(jnp.int32, (tok_rows, tok_rows), 1)
    ).astype(jnp.bfloat16)
    slot_pos = dot_f32(mine.astype(jnp.bfloat16), earlier, ((1,), (0,))).astype(jnp.int32)
    slot_ids = lax.broadcasted_iota(jnp.int32, (4, 2 * CAP, tok_rows), 1) % CAP
    picked = mine[:, None, :] & (slot_pos[:, None, :] == slot_ids)
    sel = picked.reshape(-1, tok_rows)
    other_of = jnp.sum(jnp.where(picked, other[:, None, :], 0), axis=2).reshape(-1)
    sel_bf = sel.astype(jnp.bfloat16)
    x_sel = dot_f32(sel_bf, inputs, ((1,), (0,))).astype(jnp.bfloat16)
    dy_sel = dot_f32(sel_bf, out_grad, ((1,), (0,)))
    logits = dot_f32(x_sel, router_weight, ((1,), (0,)))
    n_rows = sel.shape[0]
    lane = lax.broadcasted_iota(jnp.int32, (n_rows, n_experts), 1)
    row = lax.broadcasted_iota(jnp.int32, (n_rows, n_experts), 0)
    own_logit = jnp.sum(jnp.where(lane == row // (2 * CAP), logits, 0.0), axis=1)
    other_logit = jnp.sum(jnp.where(lane == other_of[:, None], logits, 0.0), axis=1)
    gate = 1.0 / (1.0 + jnp.exp(other_logit - own_logit))
    g_sel = (gate[:, None] * dy_sel).astype(jnp.bfloat16)
    is_x = (lax.broadcasted_iota(jnp.int32, (n_rows, 1), 0) // CAP) % 2 == 0
    return jnp.where(is_x, x_sel, g_sel), sel_bf


def gather_plane(rows):
    pieces = [rows, shift(rows, 3), shift(rows, 2), shift(rows, 1)]
    own = jnp.concatenate(pieces, axis=0)
    return own, swap(own, "core")


def row_order(n_rows, kind):
    to = lax.broadcasted_iota(jnp.int32, (n_rows, 2 * n_rows), 0)
    at = lax.broadcasted_iota(jnp.int32, (n_rows, 2 * n_rows), 1)
    core = (to // 128 - lax.axis_index("core")) & 1
    y = (to // 32 - lax.axis_index("y")) & 3
    zh = (to // 16 - lax.axis_index("zh")) & 1
    x = (to // CAP) & 3
    source = core * 256 + y * 64 + zh * 32 + x * 8 + kind * CAP + (to & (CAP - 1))
    return (at == source).astype(jnp.bfloat16)


def home_order(n_rows):
    to = lax.broadcasted_iota(jnp.int32, (n_rows, n_rows), 0)
    at = lax.broadcasted_iota(jnp.int32, (n_rows, n_rows), 1)
    zh = (to // CAP) & 1
    source = zh * 16 + to // (2 * CAP) * CAP + (to & (CAP - 1))
    return (at == source).astype(jnp.bfloat16)


def block_of(rows, begin, height):
    return lax.dynamic_slice(
        rows, (begin, 0), (height, rows.shape[1]), allow_negative_indices=False
    )


def line_sums(streams, n_group, beside, ties):
    height = streams[0].shape[0] // n_group
    top = (n_group - 1) * height
    here, core = lax.axis_index("group"), lax.axis_index("core")
    rank = jnp.where(core == 0, here, n_group - 1 - here)
    towards = height * (1 - 2 * core)
    carried, last = [None] * len(streams), streams[0]
    for step in range(n_group - 1):
        begin = lax.clamp(0, here * height + (n_group - 1 - step) * towards, top)
        reach = min((step // 4 + 1) * 4, n_group - 1)
        pairs = [(2 * i, 2 * i + 2) for i in range(reach)]
        pairs += [(2 * (n_group - 1 - i) + 1, 2 * (n_group - 2 - i) + 1) for i in range(reach)]
        for k, rows in enumerate(streams):
            term = block_of(rows, begin, height)
            if step:
                carried[k], last = lax.optimization_barrier((carried[k], last))
                term = term + jnp.where(rank <= step, carried[k], jnp.zeros_like(carried[k]))
            carried[k], last = lax.ppermute(term, ("group", "core"), pairs), term
        if step in ties:
            beside, carried[0] = lax.optimization_barrier((beside, carried[0]))
            beside = ties[step](beside)
    beside, _ = lax.optimization_barrier((beside, last))
    return carried, beside


def shards(inputs, out_grad, routes, router_weight, w_in, w_out):
    n_tok, d_model = inputs.shape
    ff_dev = w_in.shape[1]
    n_group = lax.axis_size("group")
    send, sel = slot_rows(inputs, out_grad, routes, router_weight)
    got = lax.all_to_all(send.reshape(4, 2 * CAP, d_model), "x", 0, 0, tiled=True)
    got = got.reshape(8 * CAP, d_model)
    far, order_x, order_g = lax.optimization_barrier(
        (swap(got, "zh"), row_order(64 * CAP, 0), row_order(64 * CAP, 1))
    )
    own, across = gather_plane(jnp.concatenate([got, far], axis=0))

    def in_order(order):
        half = order.shape[1] // 2
        total = dot_f32(order[:, :half], own, ((1,), (0,)))
        return (total + dot_f32(order[:, half:], across, ((1,), (0,)))).astype(jnp.bfloat16)

    x_all, g_all = in_order(order_x), in_order(order_g)
    pre_act = dot_f32(x_all, w_in, ((1,), (0,)))
    value, slope = gelu_pair(pre_act)
    hidden = value.astype(jnp.bfloat16)
    hidden_both = jnp.concatenate([hidden, swap(hidden, "core")], axis=1)
    back_hid = dot_f32(g_all, w_out, ((1,), (1,)))
    hid_grad = (back_hid * slope).astype(jnp.bfloat16)
    partial = dot_f32(hid_grad, w_in, ((1,), (1,))).astype(jnp.bfloat16)

    def product(rows, units):
        return dot_f32(rows, units, ((0,), (0,))).astype(jnp.bfloat16)

    hid_grad_both = jnp.concatenate([hid_grad, swap(hid_grad, "core")], axis=1)
    grad_out = product(g_all, hidden_both)
    grad_in = product(x_all, hid_grad_both)

    def along_y(rows):
        return lax.all_to_all(rows.reshape(4, -1, d_model), "y", 0, 0, tiled=True)

    def summed(parts):
        return jnp.sum(parts.astype(jnp.float32), axis=0).astype(jnp.bfloat16)

    def home(rows):
        parts = dot_f32(home_order(rows.shape[0]), rows, ((1,), (0,))).astype(jnp.bfloat16)
        parts = parts.reshape(8, CAP, d_model)
        return lax.all_to_all(parts, ("x", "zh"), 0, 0, tiled=True).reshape(8 * CAP, d_model)

    core, half = lax.axis_index("core"), partial.shape[0] // 2
    given = swap(block_of(partial, (1 - core) * half, half), "core").astype(jnp.float32)
    given = (block_of(partial, core * half, half).astype(jnp.float32) + given).astype(jnp.bfloat16)
    sums, slots = line_sums(
        [grad_out, grad_in], n_group, given, {0: along_y, 2: summed, 4: lambda rows: rows}
    )
    slots = home(slots)
    in_grad = dot_f32(sel, slots, ((0,), (0,))).astype(jnp.bfloat16)
    width = d_model // n_group
    here = lax.axis_index("group") * width
    across = [swap(carried[:, ff_dev:], "core") for carried in sums]

    def total(own, carried, given):
        parts = (block_of(own, here, width)[:, :ff_dev], carried[:, :ff_dev], given)
        return sum(part.astype(jnp.float32) for part in parts).astype(jnp.bfloat16)

    w_out_grad = total(grad_out, sums[0], across[0])
    w_in_grad = total(grad_in, sums[1], across[1])
    return in_grad, w_in_grad, w_out_grad.T


def solution(mesh):
    fine = Mesh(mesh.devices.reshape(SPLIT_AXES), AXES)
    everyone = ("group",) + LOCAL
    return jax.shard_map(
        shards,
        mesh=fine,
        in_specs=(
            P(everyone, None),
            P(everyone, None),
            P(everyone, None),
            P(),
            P(None, LOCAL),
            P(LOCAL, None),
        ),
        out_specs=(P(everyone, None), P("group", LOCAL), P(LOCAL, "group")),
        check_vma=False,
    )
```

```python
import jax
import jax.numpy as jnp
from jax import lax
from jax.sharding import Mesh, PartitionSpec as P

CAP = 4
SPLIT_AXES = (16, 4, 2, 4, 2)
AXES = ("group", "x", "zh", "y", "core")
LOCAL = ("x", "zh", "y", "core")

gelu_c = 0.7978845608
gelu_a = 0.044715


def gelu_pair(pre_act):
    inner = gelu_c * (pre_act + gelu_a * pre_act * pre_act * pre_act)
    tval = jnp.tanh(inner)
    value = 0.5 * pre_act * (1.0 + tval)
    slope = 0.5 * (1.0 + tval) + 0.5 * pre_act * (1.0 - tval * tval) * gelu_c * (
        1.0 + 3.0 * gelu_a * pre_act * pre_act
    )
    return (value, slope)


def dot_f32(a, b, dims):
    return lax.dot_general(a, b, (dims, ((), ())), preferred_element_type=jnp.float32)


def swap(value, axis):
    return lax.ppermute(value, axis, [(0, 1), (1, 0)])


def shift(value, by):
    return lax.ppermute(value, "y", [(i, (i + by) % 4) for i in range(4)])


def slot_rows(inputs, out_grad, routes, router_weight):
    tok_rows = inputs.shape[0]
    n_experts = router_weight.shape[1]
    first, second = routes[:, 0], routes[:, 1]
    expert = lax.broadcasted_iota(jnp.int32, (4, tok_rows), 0)
    mine = (first[None, :] == expert) | (second[None, :] == expert)
    other = jnp.where(mine, first[None, :] + second[None, :] - expert, 0)
    earlier = (
        lax.broadcasted_iota(jnp.int32, (tok_rows, tok_rows), 0)
        < lax.broadcasted_iota(jnp.int32, (tok_rows, tok_rows), 1)
    ).astype(jnp.bfloat16)
    slot_pos = dot_f32(mine.astype(jnp.bfloat16), earlier, ((1,), (0,))).astype(jnp.int32)
    slot_ids = lax.broadcasted_iota(jnp.int32, (4, 2 * CAP, tok_rows), 1) % CAP
    picked = mine[:, None, :] & (slot_pos[:, None, :] == slot_ids)
    sel = picked.reshape(-1, tok_rows)
    other_of = jnp.sum(jnp.where(picked, other[:, None, :], 0), axis=2).reshape(-1)
    sel_bf = sel.astype(jnp.bfloat16)
    x_sel = dot_f32(sel_bf, inputs, ((1,), (0,))).astype(jnp.bfloat16)
    dy_sel = dot_f32(sel_bf, out_grad, ((1,), (0,)))
    logits = dot_f32(x_sel, router_weight, ((1,), (0,)))
    n_rows = sel.shape[0]
    lane = lax.broadcasted_iota(jnp.int32, (n_rows, n_experts), 1)
    row = lax.broadcasted_iota(jnp.int32, (n_rows, n_experts), 0)
    own_logit = jnp.sum(jnp.where(lane == row // (2 * CAP), logits, 0.0), axis=1)
    other_logit = jnp.sum(jnp.where(lane == other_of[:, None], logits, 0.0), axis=1)
    gate = 1.0 / (1.0 + jnp.exp(other_logit - own_logit))
    g_sel = (gate[:, None] * dy_sel).astype(jnp.bfloat16)
    is_x = (lax.broadcasted_iota(jnp.int32, (n_rows, 1), 0) // CAP) % 2 == 0
    return jnp.where(is_x, x_sel, g_sel), sel_bf


def gather_plane(rows):
    pieces = [rows, shift(rows, 3), shift(rows, 2), shift(rows, 1)]
    own = jnp.concatenate(pieces, axis=0)
    return own, swap(own, "core")


def row_order(n_rows, kind):
    to = lax.broadcasted_iota(jnp.int32, (n_rows, 2 * n_rows), 0)
    at = lax.broadcasted_iota(jnp.int32, (n_rows, 2 * n_rows), 1)
    core = (to // 128 - lax.axis_index("core")) & 1
    y = (to // 32 - lax.axis_index("y")) & 3
    zh = (to // 16 - lax.axis_index("zh")) & 1
    x = (to // CAP) & 3
    source = core * 256 + y * 64 + zh * 32 + x * 8 + kind * CAP + (to & (CAP - 1))
    return (at == source).astype(jnp.bfloat16)


def home_order(n_rows):
    to = lax.broadcasted_iota(jnp.int32, (n_rows, n_rows), 0)
    at = lax.broadcasted_iota(jnp.int32, (n_rows, n_rows), 1)
    zh = (to // CAP) & 1
    source = zh * 16 + to // (2 * CAP) * CAP + (to & (CAP - 1))
    return (at == source).astype(jnp.bfloat16)


def block_of(rows, begin, height):
    return lax.dynamic_slice(
        rows, (begin, 0), (height, rows.shape[1]), allow_negative_indices=False
    )


def line_sums(streams, n_group, beside, ties):
    height = streams[0].shape[0] // n_group
    top = (n_group - 1) * height
    here, core = lax.axis_index("group"), lax.axis_index("core")
    rank = jnp.where(core == 0, here, n_group - 1 - here)
    towards = height * (1 - 2 * core)
    carried, last = [None] * len(streams), streams[0]
    for step in range(n_group - 1):
        begin = lax.clamp(0, here * height + (n_group - 1 - step) * towards, top)
        reach = min((step // 2 + 1) * 2, n_group - 1)
        pairs = [(2 * i, 2 * i + 2) for i in range(reach)]
        pairs += [(2 * (n_group - 1 - i) + 1, 2 * (n_group - 2 - i) + 1) for i in range(reach)]
        for k, rows in enumerate(streams):
            term = block_of(rows, begin, height)
            if step:
                carried[k], last = lax.optimization_barrier((carried[k], last))
                term = term + jnp.where(rank <= step, carried[k], jnp.zeros_like(carried[k]))
            carried[k], last = lax.ppermute(term, ("group", "core"), pairs), term
        if step in ties:
            beside, carried[0] = lax.optimization_barrier((beside, carried[0]))
            beside = ties[step](beside)
    return carried, beside


def shards(inputs, out_grad, routes, router_weight, w_in, w_out):
    n_tok, d_model = inputs.shape
    ff_dev = w_in.shape[1]
    n_group = lax.axis_size("group")
    send, sel = slot_rows(inputs, out_grad, routes, router_weight)
    got = lax.all_to_all(send.reshape(4, 2 * CAP, d_model), "x", 0, 0, tiled=True)
    got = got.reshape(8 * CAP, d_model)
    far, order_x, order_g = lax.optimization_barrier(
        (swap(got, "zh"), row_order(64 * CAP, 0), row_order(64 * CAP, 1))
    )
    own, across = gather_plane(jnp.concatenate([got, far], axis=0))

    def in_order(order):
        half = order.shape[1] // 2
        total = dot_f32(order[:, :half], own, ((1,), (0,)))
        return (total + dot_f32(order[:, half:], across, ((1,), (0,)))).astype(jnp.bfloat16)

    x_all, g_all = in_order(order_x), in_order(order_g)
    pre_act = dot_f32(x_all, w_in, ((1,), (0,)))
    value, slope = gelu_pair(pre_act)
    hidden = value.astype(jnp.bfloat16)
    hidden_both = jnp.concatenate([hidden, swap(hidden, "core")], axis=1)
    back_hid = dot_f32(g_all, w_out, ((1,), (1,)))
    hid_grad = (back_hid * slope).astype(jnp.bfloat16)
    partial = dot_f32(hid_grad, w_in, ((1,), (1,))).astype(jnp.bfloat16)

    def product(rows, units):
        return dot_f32(rows, units, ((0,), (0,))).astype(jnp.bfloat16)

    hid_grad_both = jnp.concatenate([hid_grad, swap(hid_grad, "core")], axis=1)
    grad_out = product(g_all, hidden_both)
    grad_in = product(x_all, hid_grad_both)

    def along_y(rows):
        return lax.all_to_all(rows.reshape(4, -1, d_model), "y", 0, 0, tiled=True)

    def summed(parts):
        return jnp.sum(parts.astype(jnp.float32), axis=0).astype(jnp.bfloat16)

    def home(rows):
        parts = dot_f32(home_order(rows.shape[0]), rows, ((1,), (0,))).astype(jnp.bfloat16)
        parts = parts.reshape(8, CAP, d_model)
        return lax.all_to_all(parts, ("x", "zh"), 0, 0, tiled=True).reshape(8 * CAP, d_model)

    core, half = lax.axis_index("core"), partial.shape[0] // 2
    given = swap(block_of(partial, (1 - core) * half, half), "core").astype(jnp.float32)
    given = (block_of(partial, core * half, half).astype(jnp.float32) + given).astype(jnp.bfloat16)
    sums, slots = line_sums(
        [grad_out, grad_in], n_group, given, {0: along_y, 1: lambda parts: home(summed(parts)), 4: lambda rows: rows}
    )
    in_grad = dot_f32(sel, slots, ((0,), (0,))).astype(jnp.bfloat16)
    width = d_model // n_group
    here = lax.axis_index("group") * width
    across = [swap(carried[:, ff_dev:], "core") for carried in sums]

    def total(own, carried, given):
        parts = (block_of(own, here, width)[:, :ff_dev], carried[:, :ff_dev], given)
        return sum(part.astype(jnp.float32) for part in parts).astype(jnp.bfloat16)

    w_out_grad = total(grad_out, sums[0], across[0])
    w_in_grad = total(grad_in, sums[1], across[1])
    return in_grad, w_in_grad, w_out_grad.T


def solution(mesh):
    fine = Mesh(mesh.devices.reshape(SPLIT_AXES), AXES)
    everyone = ("group",) + LOCAL
    return jax.shard_map(
        shards,
        mesh=fine,
        in_specs=(
            P(everyone, None),
            P(everyone, None),
            P(everyone, None),
            P(),
            P(None, LOCAL),
            P(LOCAL, None),
        ),
        out_specs=(P(everyone, None), P("group", LOCAL), P(LOCAL, "group")),
        check_vma=False,
    )
```

```python
import jax
import jax.numpy as jnp
from jax import lax
from jax.sharding import Mesh, PartitionSpec as P

CAP = 4
SPLIT_AXES = (16, 4, 2, 4, 2)
AXES = ("group", "x", "zh", "y", "core")
LOCAL = ("x", "zh", "y", "core")

gelu_c = 0.7978845608
gelu_a = 0.044715


def gelu_pair(pre_act):
    inner = gelu_c * (pre_act + gelu_a * pre_act * pre_act * pre_act)
    tval = jnp.tanh(inner)
    value = 0.5 * pre_act * (1.0 + tval)
    slope = 0.5 * (1.0 + tval) + 0.5 * pre_act * (1.0 - tval * tval) * gelu_c * (
        1.0 + 3.0 * gelu_a * pre_act * pre_act
    )
    return (value, slope)


def dot_f32(a, b, dims):
    return lax.dot_general(a, b, (dims, ((), ())), preferred_element_type=jnp.float32)


def swap(value, axis):
    return lax.ppermute(value, axis, [(0, 1), (1, 0)])


def shift(value, by):
    return lax.ppermute(value, "y", [(i, (i + by) % 4) for i in range(4)])


def slot_rows(inputs, out_grad, routes, router_weight):
    tok_rows = inputs.shape[0]
    n_experts = router_weight.shape[1]
    first, second = routes[:, 0], routes[:, 1]
    expert = lax.broadcasted_iota(jnp.int32, (4, tok_rows), 0)
    mine = (first[None, :] == expert) | (second[None, :] == expert)
    other = jnp.where(mine, first[None, :] + second[None, :] - expert, 0)
    earlier = (
        lax.broadcasted_iota(jnp.int32, (tok_rows, tok_rows), 0)
        < lax.broadcasted_iota(jnp.int32, (tok_rows, tok_rows), 1)
    ).astype(jnp.bfloat16)
    slot_pos = dot_f32(mine.astype(jnp.bfloat16), earlier, ((1,), (0,))).astype(jnp.int32)
    slot_ids = lax.broadcasted_iota(jnp.int32, (4, 2 * CAP, tok_rows), 1) % CAP
    picked = mine[:, None, :] & (slot_pos[:, None, :] == slot_ids)
    sel = picked.reshape(-1, tok_rows)
    other_of = jnp.sum(jnp.where(picked, other[:, None, :], 0), axis=2).reshape(-1)
    sel_bf = sel.astype(jnp.bfloat16)
    x_sel = dot_f32(sel_bf, inputs, ((1,), (0,))).astype(jnp.bfloat16)
    dy_sel = dot_f32(sel_bf, out_grad, ((1,), (0,)))
    logits = dot_f32(x_sel, router_weight, ((1,), (0,)))
    n_rows = sel.shape[0]
    lane = lax.broadcasted_iota(jnp.int32, (n_rows, n_experts), 1)
    row = lax.broadcasted_iota(jnp.int32, (n_rows, n_experts), 0)
    own_logit = jnp.sum(jnp.where(lane == row // (2 * CAP), logits, 0.0), axis=1)
    other_logit = jnp.sum(jnp.where(lane == other_of[:, None], logits, 0.0), axis=1)
    gate = 1.0 / (1.0 + jnp.exp(other_logit - own_logit))
    g_sel = (gate[:, None] * dy_sel).astype(jnp.bfloat16)
    is_x = (lax.broadcasted_iota(jnp.int32, (n_rows, 1), 0) // CAP) % 2 == 0
    return jnp.where(is_x, x_sel, g_sel), sel_bf


def gather_plane(rows):
    pieces = [rows, shift(rows, 3), shift(rows, 2), shift(rows, 1)]
    own = jnp.concatenate(pieces, axis=0)
    return own, swap(own, "core")


def row_order(n_rows, kind):
    to = lax.broadcasted_iota(jnp.int32, (n_rows, 2 * n_rows), 0)
    at = lax.broadcasted_iota(jnp.int32, (n_rows, 2 * n_rows), 1)
    core = (to // 128 - lax.axis_index("core")) & 1
    y = (to // 32 - lax.axis_index("y")) & 3
    zh = (to // 16 - lax.axis_index("zh")) & 1
    x = (to // CAP) & 3
    source = core * 256 + y * 64 + zh * 32 + x * 8 + kind * CAP + (to & (CAP - 1))
    return (at == source).astype(jnp.bfloat16)


def home_order(n_rows):
    to = lax.broadcasted_iota(jnp.int32, (n_rows, n_rows), 0)
    at = lax.broadcasted_iota(jnp.int32, (n_rows, n_rows), 1)
    zh = (to // CAP) & 1
    source = zh * 16 + to // (2 * CAP) * CAP + (to & (CAP - 1))
    return (at == source).astype(jnp.bfloat16)


def block_of(rows, begin, height):
    return lax.dynamic_slice(
        rows, (begin, 0), (height, rows.shape[1]), allow_negative_indices=False
    )


def line_sums(streams, n_group, beside, ties):
    height = streams[0].shape[0] // n_group
    top = (n_group - 1) * height
    here, core = lax.axis_index("group"), lax.axis_index("core")
    rank = jnp.where(core == 0, here, n_group - 1 - here)
    towards = height * (1 - 2 * core)
    carried, last = [None] * len(streams), streams[0]
    for step in range(n_group - 1):
        begin = lax.clamp(0, here * height + (n_group - 1 - step) * towards, top)
        reach = min((step // 2 + 1) * 2, n_group - 1)
        pairs = [(2 * i, 2 * i + 2) for i in range(reach)]
        pairs += [(2 * (n_group - 1 - i) + 1, 2 * (n_group - 2 - i) + 1) for i in range(reach)]
        for k, rows in enumerate(streams):
            term = block_of(rows, begin, height)
            if step:
                carried[k], last = lax.optimization_barrier((carried[k], last))
                term = term + jnp.where(rank <= step, carried[k], jnp.zeros_like(carried[k]))
            carried[k], last = lax.ppermute(term, ("group", "core"), pairs), term
        if step in ties:
            beside, carried[0] = lax.optimization_barrier((beside, carried[0]))
            beside = ties[step](beside)
    return carried, beside


def shards(inputs, out_grad, routes, router_weight, w_in, w_out):
    n_tok, d_model = inputs.shape
    ff_dev = w_in.shape[1]
    n_group = lax.axis_size("group")
    send, sel = slot_rows(inputs, out_grad, routes, router_weight)
    got = lax.all_to_all(send.reshape(4, 2 * CAP, d_model), "x", 0, 0, tiled=True)
    got = got.reshape(8 * CAP, d_model)
    far, order_x, order_g = lax.optimization_barrier(
        (swap(got, "zh"), row_order(64 * CAP, 0), row_order(64 * CAP, 1))
    )
    own, across = gather_plane(jnp.concatenate([got, far], axis=0))

    rows = jnp.concatenate(lax.optimization_barrier((own, across)), axis=0)
    x_all = dot_f32(order_x, rows, ((1,), (0,))).astype(jnp.bfloat16)
    g_all = dot_f32(order_g, rows, ((1,), (0,))).astype(jnp.bfloat16)
    pre_act = dot_f32(x_all, w_in, ((1,), (0,)))
    value, slope = gelu_pair(pre_act)
    hidden = value.astype(jnp.bfloat16)
    hidden_both = jnp.concatenate([hidden, swap(hidden, "core")], axis=1)
    back_hid = dot_f32(g_all, w_out, ((1,), (1,)))
    hid_grad = (back_hid * slope).astype(jnp.bfloat16)
    partial = dot_f32(hid_grad, w_in, ((1,), (1,))).astype(jnp.bfloat16)

    def product(rows, units):
        return dot_f32(rows, units, ((0,), (0,))).astype(jnp.bfloat16)

    hid_grad_both = jnp.concatenate([hid_grad, swap(hid_grad, "core")], axis=1)
    grad_out = product(g_all, hidden_both)
    grad_in = product(x_all, hid_grad_both)

    def along_y(rows):
        return lax.all_to_all(rows.reshape(4, -1, d_model), "y", 0, 0, tiled=True)

    def summed(parts):
        return jnp.sum(parts.astype(jnp.float32), axis=0).astype(jnp.bfloat16)

    def home(rows):
        parts = dot_f32(home_order(rows.shape[0]), rows, ((1,), (0,))).astype(jnp.bfloat16)
        parts = parts.reshape(8, CAP, d_model)
        return lax.all_to_all(parts, ("x", "zh"), 0, 0, tiled=True).reshape(8 * CAP, d_model)

    core, half = lax.axis_index("core"), partial.shape[0] // 2
    given = swap(block_of(partial, (1 - core) * half, half), "core").astype(jnp.float32)
    given = (block_of(partial, core * half, half).astype(jnp.float32) + given).astype(jnp.bfloat16)
    sums, slots = line_sums(
        [grad_out, grad_in], n_group, given, {0: along_y, 1: lambda parts: home(summed(parts)), 4: lambda rows: rows}
    )
    in_grad = dot_f32(sel, slots, ((0,), (0,))).astype(jnp.bfloat16)
    width = d_model // n_group
    here = lax.axis_index("group") * width
    across = [swap(carried[:, ff_dev:], "core") for carried in sums]

    def total(own, carried, given):
        parts = (block_of(own, here, width)[:, :ff_dev], carried[:, :ff_dev], given)
        return sum(part.astype(jnp.float32) for part in parts).astype(jnp.bfloat16)

    w_out_grad = total(grad_out, sums[0], across[0])
    w_in_grad = total(grad_in, sums[1], across[1])
    return in_grad, w_in_grad, w_out_grad.T


def solution(mesh):
    fine = Mesh(mesh.devices.reshape(SPLIT_AXES), AXES)
    everyone = ("group",) + LOCAL
    return jax.shard_map(
        shards,
        mesh=fine,
        in_specs=(
            P(everyone, None),
            P(everyone, None),
            P(everyone, None),
            P(),
            P(None, LOCAL),
            P(LOCAL, None),
        ),
        out_specs=(P(everyone, None), P("group", LOCAL), P(LOCAL, "group")),
        check_vma=False,
    )
```
